256 devices in a mesh: outer: 8 (over x_hi, y), inner: 32 (over x_lo, z, core).
Axes of the slice: x: 4 (x_hi: 2, x_lo: 2; x = x_hi * 2 + x_lo), y: 4, z: 8, core: 2. Of those that a mesh axis runs over, the one named last changes fastest.
Arguments:
- queries: bfloat16 [32768, 512], P(('outer', 'inner')), may hold values from -24 to 24
- keys: bfloat16 [32768, 512], P(('outer', 'inner')), may hold values from -24 to 24
- values: bfloat16 [32768, 512], P(('outer', 'inner')), may hold values from -6 to 6
- block_pos: int32 [256], P(('outer', 'inner')), may hold values from 0 to 255, each once
Outputs:
- attended: bfloat16 [32768, 512], P(('outer', 'inner'))
The draws below stay inside these ranges and needn't reach their ends.
All inputs are finite; a program needn't handle non-finite values.
Results may differ from the reference program's by a relative error of at most 0.009.
Values may be sent and summed in bfloat16 or wider, within the bound.
A program may use at most 192 MiB of HBM per device.

```python
import math
import jax
import jax.numpy as jnp
from jax import lax

HEADS = 4
HEAD_DIM = 128
TOK_DEV = 128
BLOCKS = 256
TOKENS = 32768


def shared_keys(key):
    width = HEADS * HEAD_DIM
    return jax.random.truncated_normal(key, -6.0, 6.0, (TOKENS, width), jnp.float32)


def draw_keys(key, part):
    base = shared_keys(key)
    return base.astype(jnp.bfloat16)


def draw_queries(key, part):
    key = jax.random.fold_in(key, 5)
    width = HEADS * HEAD_DIM
    fresh = jax.random.truncated_normal(key, -6.0, 6.0, (TOKENS, width), jnp.float32)
    return fresh.astype(jnp.bfloat16)


def levels(key, shape, shards, least, top_value):
    gain, own = 1.0, jax.random.fold_in(key, 6)
    for axis_at, blocks in shards:
        draws = jnp.exp(jax.random.uniform(jax.random.fold_in(own, axis_at), (blocks,), jnp.float32, least / len(shards), top_value / len(shards)))
        gain = gain * jnp.repeat(draws, shape[axis_at] // blocks).reshape([-1 if axis == axis_at else 1 for axis in range(len(shape))])
    return gain


def bell_draw(own_key, shape, scale, limit, cuts=(), kind=jnp.bfloat16):
    values = jax.random.normal(own_key, shape, jnp.float32) * scale
    if len(cuts) > 0:
        values = levels(own_key, shape, cuts, -0.22, 0.18) * values
    return jnp.clip(values, min=-limit, max=limit).astype(kind)


def setup_inputs(seed: int = 0) -> dict:
    splits = jax.random.split(jax.random.key(seed), 5)
    return {
        "queries": draw_queries(jax.random.fold_in(splits[4], 71), 0),
        "keys": draw_keys(jax.random.fold_in(splits[4], 71), 0),
        "values": bell_draw(splits[2], (TOKENS, HEADS * HEAD_DIM), 1.0, 6.0, ((0, 256),)),
        "block_pos": jax.random.permutation(splits[3], BLOCKS).astype(jnp.int32),
    }


def reference(queries, keys, values, block_pos):
    width = HEADS * HEAD_DIM
    nblk = block_pos.shape[0]
    order = jnp.argsort(block_pos).astype(jnp.int32)
    q_sorted = queries.reshape(nblk, TOK_DEV, width)[order].reshape(TOKENS, width)
    k_sorted = keys.reshape(nblk, TOK_DEV, width)[order].reshape(TOKENS, width)
    v_sorted = values.reshape(nblk, TOK_DEV, width)[order].reshape(TOKENS, width)
    span = math.gcd(TOKENS, 1024)
    scale = HEAD_DIM ** -0.5

    def one_block(qi):
        qrows = lax.dynamic_slice_in_dim(q_sorted, qi * span, span, 0).astype(jnp.float32).reshape(span, HEADS, HEAD_DIM)
        qpos = qi * span + jnp.arange(span, dtype=jnp.int32)

        def step(kj, carry):
            acc, top, total = carry
            krows = lax.dynamic_slice_in_dim(k_sorted, kj * span, span, 0).astype(jnp.float32).reshape(span, HEADS, HEAD_DIM)
            vrows = lax.dynamic_slice_in_dim(v_sorted, kj * span, span, 0).astype(jnp.float32).reshape(span, HEADS, HEAD_DIM)
            kpos = kj * span + jnp.arange(span, dtype=jnp.int32)
            scores = jnp.einsum("qhd,khd->hqk", qrows, krows) * scale
            allowed = kpos[None, :] <= qpos[:, None]
            scores = jnp.where(allowed[None], scores, -1e30)
            newtop = jnp.maximum(top, jnp.max(scores, axis=-1))
            weights = jnp.where(allowed[None], jnp.exp(scores - newtop[..., None]), 0.0).astype(jnp.bfloat16)
            factor = jnp.exp(top - newtop)
            wide = weights.astype(jnp.float32)
            total = total * factor + jnp.sum(wide, axis=-1)
            acc = acc * factor.T[:, :, None] + jnp.einsum("hqk,khd->qhd", wide, vrows)
            return acc, newtop, total

        init = (jnp.zeros((span, HEADS, HEAD_DIM), jnp.float32), jnp.full((HEADS, span), -1e30, jnp.float32), jnp.zeros((HEADS, span), jnp.float32))
        acc, top, total = lax.fori_loop(0, qi + 1, step, init)
        return (acc / total.T[:, :, None]).reshape(span, width).astype(jnp.bfloat16)

    outs = lax.map(one_block, jnp.arange(TOKENS // span, dtype=jnp.int32))
    sorted_out = outs.reshape(nblk, TOK_DEV, width)
    return sorted_out[block_pos].reshape(TOKENS, width)
```

```python
import functools

import jax
import jax.numpy as jnp
from jax import lax
from jax.experimental import pallas as pl
from jax.experimental.pallas import tpu as pltpu
from jax.sharding import PartitionSpec as P

TOK = 128
DIM = 128
SUP = 4 * TOK
TQ = 1024
TK = SUP
ROWS = DIM + 16
NQ = 8 * SUP
NK = 8 * SUP
SCALE = DIM**-0.5 * 1.4426950408889634
LOW = -1e30
MESH = pl.DeviceIdType.MESH

OFFSETS = ((0, 0), (0, 1), (0, 3), (0, 2), (1, 0), (1, 1), (1, 3), (1, 2))
BACK = (0, 2, 1, 3, 4, 6, 5, 7)

KEYS_AT = {1: 3, 2: 3, 3: 11, 4: 11, 5: 19, 6: 19, 7: 21}
VALS_AT = {1: 5, 2: 5, 3: 13, 4: 13, 5: 21, 6: 21, 7: 23}
OUTER_SLOTS = 5
TILES = NQ // TQ
LAST_SLOTS = 8 - OUTER_SLOTS
STEPS = 8 * TILES


def kernel(
    q_in, k_in, v_in, p_in, out_ref,
    qall, kall, vall, qpos, kpos, vt, ptile, acc, mx,
    cm_a, cm_b, al_a, al_b, s_a, s_b, p_a, p_b,
    osend, ssend, orecv, srecv, fsend, frecv,
    cell_s, cell_r, ring_s, ring_r, q_s, q_r, o_s, o_r, f_s, f_r,
):
    o, i = lax.axis_index("outer"), lax.axis_index("inner")
    xh, y = o // 4, lax.rem(o, 4)
    xl, z, core = i // 16, lax.rem(i // 2, 8), lax.rem(i, 2)
    me = xl * 2 + core

    def cell(b):
        return (o, (b // 2) * 16 + z * 2 + lax.rem(b, 2))

    def ring(step):
        return (o, xl * 16 + lax.rem(z + step, 8) * 2 + core)

    def group(slot):
        dx, dy = OFFSETS[slot]
        return (lax.rem(xh + dx, 2) * 4 + lax.rem(y + dy, 4), i)

    def lanes(b):
        return pl.ds(pl.multiple_of(b * TOK, TOK), TOK)

    def remote(src, dst, send, recv, device):
        return pltpu.make_async_remote_copy(
            src_ref=src, dst_ref=dst, send_sem=send, recv_sem=recv, device_id=device, device_id_type=MESH
        )

    barrier = pltpu.get_barrier_semaphore()
    partners = [cell(lax.rem(me + j, 4)) for j in (1, 2, 3)] + [ring(1), ring(7)] + [group(s) for s in range(1, 8)]
    for partner in partners:
        pl.semaphore_signal(barrier, inc=1, device_id=partner, device_id_type=MESH)
    ptile[...] = jnp.full(ptile.shape, p_in[0], jnp.int32)
    for h in range(4):
        vt[h * DIM : (h + 1) * DIM, :] = v_in[:, h * DIM : (h + 1) * DIM].T
    pl.semaphore_wait(barrier, len(partners))

    def trade(j, what, block):
        to = lax.rem(me + j, 4)
        src, dst = (
            (k_in.at[:, lanes(to)], kall.at[lanes(block), :]),
            (ptile, kpos.at[:, lanes(block)]),
            (q_in.at[:, lanes(to)], qall.at[lanes(block), :]),
            (vt.at[lanes(to), :], vall.at[pl.ds(0, DIM), lanes(block)]),
        )[what]
        return remote(src, dst, cell_s.at[j - 1, what], cell_r.at[j - 1, what], cell(to))

    for what in range(4):
        for j in (2, 1, 3):
            trade(j, what, me).start()

    own = lanes(me)
    kall[own, :] = k_in[:, own]
    kpos[:, own] = ptile[...]
    qall[own, :] = q_in[:, own]
    vall[0:DIM, own] = vt[own, :]
    vall[DIM:, :] = jnp.ones((ROWS - DIM, NK), jnp.bfloat16)

    def traded(what):
        for j in (1, 2, 3):
            trade(j, what, lax.rem(me + 4 - j, 4)).wait_recv()

    def hop(way, dist, what):
        if way == 0:
            src, dst = (0 if dist == 1 else 2 * dist - 3), 2 * dist - 1
        else:
            src, dst = 2 * (dist - 1), min(2 * dist, 7)
        a, b = slice(src * SUP, (src + 1) * SUP), slice(dst * SUP, (dst + 1) * SUP)
        refs = (
            (kall.at[a, :], kall.at[b, :]),
            (vall.at[0:DIM, a], vall.at[0:DIM, b]),
            (kpos.at[:, a], kpos.at[:, b]),
        )[what]
        return remote(*refs, ring_s.at[way, dist - 1, what], ring_r.at[way, dist - 1, what], ring(1 if way == 0 else 7))

    def arrival(slot):
        if slot == 7:
            return (0, 4), (1, 4)
        way = (slot + 1) % 2
        return ((way, (slot + 1) // 2),) * 2

    def keys_here(slot):
        way, dist = arrival(slot)[0]
        hop(way, dist, 0).wait_recv()
        hop(way, dist, 2).wait_recv()
        if dist < 3 or (dist == 3 and way == 0):
            hop(way, dist + 1, 0).start()
            hop(way, dist + 1, 2).start()

    def vals_here(slot):
        way, dist = arrival(slot)[1]
        hop(way, dist, 1).wait_recv()
        if dist < 3 or (dist == 3 and way == 1):
            hop(way, dist + 1, 1).start()

    def give(slot, at):
        a, b = slice(0, SUP), slice(at * SUP, (at + 1) * SUP)
        device = group(slot)
        return (
            remote(qall.at[a, :], qall.at[b, :], q_s.at[slot, 0], q_r.at[at, 0], device),
            remote(kpos.at[:, a], qpos.at[:, b], q_s.at[slot, 1], q_r.at[at, 1], device),
        )

    traded(0)
    traded(1)
    for way in range(2):
        hop(way, 1, 0).start()
        hop(way, 1, 2).start()
    traded(2)
    for slot in range(1, 8):
        for copy in give(slot, BACK[slot]):
            copy.start()
    traded(3)
    for way in range(2):
        hop(way, 1, 1).start()

    def queries_here(tile):
        for slot in range(tile * 2, tile * 2 + 2):
            if slot > 0:
                for copy in give(slot, slot):
                    copy.wait_recv()

    qpos[:, 0:SUP] = kpos[:, 0:SUP]
    acc[:, SUP:] = jnp.zeros((ROWS, NQ - SUP), jnp.float32)
    mx[:, SUP:] = jnp.full((8, NQ - SUP), LOW, jnp.float32)
    causal = lax.broadcasted_iota(jnp.int32, (TOK, TOK), 0) <= lax.broadcasted_iota(jnp.int32, (TOK, TOK), 1)
    for b in range(4):
        at = slice(b * TOK, (b + 1) * TOK)
        s = lax.dot_general(kall[at, :], qall[at, :], (((1,), (1,)), ((), ())), preferred_element_type=jnp.float32)
        s = jnp.where(causal, s, LOW)
        top = jnp.max(s, axis=0, keepdims=True)
        w = jnp.where(causal, jnp.exp2(s * SCALE - top * SCALE), 0.0).astype(jnp.bfloat16)
        acc[:, at] = jnp.dot(vall[:, at], w, preferred_element_type=jnp.float32)
        mx[:, at] = jnp.broadcast_to(top, (8, TOK))

    S, W, CM, AL = (s_a, s_b), (p_a, p_b), (cm_a, cm_b), (al_a, al_b)
    first = OUTER_SLOTS * TILES

    def place(n):
        m = jnp.maximum(n - first, 0)
        early = n < first
        slot = jnp.where(early, n // TILES, OUTER_SLOTS + lax.rem(m, LAST_SLOTS))
        tile = jnp.where(early, lax.rem(n, TILES), TILES - 1 - m // LAST_SLOTS)
        return pl.multiple_of(slot * TK, TK), pl.multiple_of(tile * TQ, TQ)

    def kept(k0, q0, t, kb):
        kp = kpos[:, pl.ds(k0 + kb * TOK, TOK)]
        return jnp.concatenate([kp] * 4, axis=1) < qpos[:, pl.ds(q0 + t * SUP, SUP)]

    def scores(n, par):
        k0, q0 = place(n)
        for t in range(TQ // SUP):
            s = lax.dot_general(
                kall[pl.ds(k0, TK), :], qall[pl.ds(q0 + t * SUP, SUP), :],
                (((1,), (1,)), ((), ())), preferred_element_type=jnp.float32,
            )
            S[par][:, t * SUP : (t + 1) * SUP] = s
            best = None
            for kb in range(TK // TOK):
                r = jnp.max(s[kb * TOK : (kb + 1) * TOK].reshape(TOK // 8, 8, SUP), axis=0)
                r = jnp.where(kept(k0, q0, t, kb), r, LOW)
                best = r if best is None else jnp.maximum(best, r)
            CM[par][:, t * SUP : (t + 1) * SUP] = best

    def weights(n, par):
        k0, q0 = place(n)
        qs = pl.ds(q0, TQ)
        old = mx[:, qs]
        new = jnp.maximum(old, jnp.max(CM[par][...], axis=0, keepdims=True))
        mx[:, qs] = new
        AL[par][...] = jnp.exp2((old - new) * SCALE)
        top = new * SCALE
        for t in range(TQ // SUP):
            ts = slice(t * SUP, (t + 1) * SUP)
            for kb in range(TK // TOK):
                less = jnp.where(kept(k0, q0, t, kb), top[:, ts], -LOW)
                ks = slice(kb * TOK, (kb + 1) * TOK)
                e = (S[par][ks, ts] * SCALE).reshape(TOK // 8, 8, SUP) - less[None]
                W[par][ks, ts] = jnp.exp2(e).reshape(TOK, SUP).astype(jnp.bfloat16)

    def sums(n, par):
        k0, q0 = place(n)
        for t in range(TQ // SUP):
            ts = slice(t * SUP, (t + 1) * SUP)
            qs = pl.ds(q0 + t * SUP, SUP)
            new = jnp.dot(vall[:, pl.ds(k0, TK)], W[par][:, ts], preferred_element_type=jnp.float32)
            acc[:, qs] = acc[:, qs] * AL[par][:1, ts] + new

    def stats(slot):
        at = slice(slot * SUP, (slot + 1) * SUP)
        m, l = mx[0:1, at], acc[DIM : DIM + 1, at]
        cut = [slice(b * TOK, (b + 1) * TOK) for b in range(4)]
        return jnp.concatenate([m[:, c] for c in cut] + [l[:, c] for c in cut], axis=0)

    def partial(slot, at):
        device = group(slot)
        return (
            remote(osend.at[slot], orecv.at[at], o_s.at[slot, 0], o_r.at[at, 0], device),
            remote(ssend.at[slot], srecv.at[at], o_s.at[slot, 1], o_r.at[at, 1], device),
        )

    def send_partial(tile):
        for slot in (tile * 2 + 1, tile * 2):
            if slot > 0:
                osend[slot] = acc[0:DIM, slot * SUP : (slot + 1) * SUP].astype(jnp.bfloat16)
                ssend[slot] = stats(slot)
                for copy in partial(slot, BACK[slot]):
                    copy.start()

    queries_here(0)
    scores(jnp.int32(0), 0)
    p_b[...] = jnp.zeros_like(p_b)
    al_b[...] = jnp.ones_like(al_b)
    done = {first + (TILES - t) * LAST_SLOTS: t for t in range(1, TILES)}

    def before(n, n_of):
        events = {}
        for slot, at in KEYS_AT.items():
            events.setdefault(at, []).append(functools.partial(keys_here, slot))
        for slot, at in VALS_AT.items():
            events.setdefault(at, []).append(functools.partial(vals_here, slot))
        for tile in range(1, TILES):
            events.setdefault(tile - 1, []).append(functools.partial(queries_here, tile))
        for at, calls in sorted(events.items()):
            if at % 2 == n_of:

                @pl.when(n == at)
                def _(calls=calls):
                    for call in calls:
                        call()

    def after(n, n_of):
        for at, tile in done.items():
            if at % 2 == n_of:

                @pl.when(n == at)
                def _(tile=tile):
                    send_partial(tile)

    def body(pair, carry):
        for par in range(2):
            n = 2 * pair + par
            before(n, par)
            scores(jnp.minimum(n + 1, STEPS - 1), 1 - par)
            weights(n, par)
            sums(jnp.maximum(n - 1, 0), 1 - par)
            after(n, par)
        return carry

    lax.fori_loop(0, STEPS // 2, body, 0)
    sums(jnp.int32(STEPS - 1), 1)
    send_partial(0)

    mine = stats(0)
    for slot in range(1, 8):
        for copy in partial(slot, slot):
            copy.wait_recv()
    all_stats = [mine] + [srecv[slot] for slot in range(1, 8)]
    best = functools.reduce(jnp.maximum, [st[0:4] for st in all_stats])
    factor = [jnp.exp2((st[0:4] - best) * SCALE) for st in all_stats]
    denom = functools.reduce(jnp.add, [st[4:8] * f for st, f in zip(all_stats, factor)])
    factor = [f / denom for f in factor]
    for b in range(4):
        at = slice(b * TOK, (b + 1) * TOK)
        total = acc[0:DIM, at] * factor[0][b : b + 1]
        for slot in range(1, 8):
            total += orecv[slot, :, at].astype(jnp.float32) * factor[slot][b : b + 1]
        fsend[b] = total.T.astype(jnp.bfloat16)

    def home(j, block):
        to = lax.rem(me + j, 4)
        return remote(fsend.at[to], frecv.at[block], f_s.at[j - 1], f_r.at[j - 1], cell(to))

    for j in (2, 1, 3):
        home(j, me).start()
    out_ref[:, own] = fsend[me]
    for j in (1, 2, 3):
        source = lax.rem(me + 4 - j, 4)
        home(j, source).wait_recv()
        out_ref[:, lanes(source)] = frecv[source]

    for j in (1, 2, 3):
        for what in range(4):
            trade(j, what, me).wait_send()
        home(j, me).wait_send()
    for way in range(2):
        for dist in range(1, 5):
            for what in range(3):
                if dist < 4 or (what == 1) == (way == 1):
                    hop(way, dist, what).wait_send()
    for slot in range(1, 8):
        for copy in give(slot, BACK[slot]) + partial(slot, BACK[slot]):
            copy.wait_send()


def shards(queries, keys, values, block_pos):
    bf, f32, i32 = jnp.bfloat16, jnp.float32, jnp.int32
    vmem, dma = pltpu.VMEM, pltpu.SemaphoreType.DMA
    return pl.pallas_call(
        kernel,
        out_shape=jax.ShapeDtypeStruct(queries.shape, bf),
        in_specs=[pl.BlockSpec(memory_space=pltpu.VMEM)] * 3 + [pl.BlockSpec(memory_space=pltpu.SMEM)],
        out_specs=pl.BlockSpec(memory_space=pltpu.VMEM),
        scratch_shapes=[
            vmem((NQ, DIM), bf), vmem((NK, DIM), bf), vmem((ROWS, NK), bf), vmem((8, NQ), i32), vmem((8, NK), i32),
            vmem((4 * DIM, TOK), bf), vmem((8, TOK), i32), vmem((ROWS, NQ), f32), vmem((8, NQ), f32),
            vmem((8, TQ), f32), vmem((8, TQ), f32), vmem((8, TQ), f32), vmem((8, TQ), f32),
            vmem((TK, TQ), f32), vmem((TK, TQ), f32), vmem((TK, TQ), bf), vmem((TK, TQ), bf),
            vmem((8, DIM, SUP), bf), vmem((8, 8, TOK), f32), vmem((8, DIM, SUP), bf), vmem((8, 8, TOK), f32),
            vmem((4, TOK, DIM), bf), vmem((4, TOK, DIM), bf),
            dma((3, 4)), dma((3, 4)), dma((2, 4, 3)), dma((2, 4, 3)), dma((8, 2)), dma((8, 2)), dma((8, 2)), dma((8, 2)),
            dma((3,)), dma((3,)),
        ],
        compiler_params=pltpu.CompilerParams(collective_id=0, has_side_effects=True, vmem_limit_bytes=56 << 20),
        cost_estimate=pl.CostEstimate(flops=NQ * NK * DIM * 4, bytes_accessed=1 << 20, transcendentals=NQ * NK),
        name="attend",
    )(queries, keys, values, block_pos)


def solution(mesh):
    spec = P(("outer", "inner"), None)
    return jax.shard_map(
        shards, mesh=mesh, in_specs=(spec, spec, spec, P(("outer", "inner"))), out_specs=spec, check_vma=False
    )
```

```python
import functools

import jax
import jax.numpy as jnp
from jax import lax
from jax.experimental import pallas as pl
from jax.experimental.pallas import tpu as pltpu
from jax.sharding import PartitionSpec as P

TOK = 128
DIM = 128
SUP = 4 * TOK
TQ = 1024
TK = 1024
ROWS = DIM + 16
NQ = 8 * SUP
NK = 8 * SUP
SCALE = DIM**-0.5 * 1.4426950408889634
LOW = -1e30
MESH = pl.DeviceIdType.MESH

OFFSETS = ((0, 0), (0, 1), (0, 3), (0, 2), (1, 0), (1, 1), (1, 3), (1, 2))
BACK = (0, 2, 1, 3, 4, 6, 5, 7)

OWN = 7
K_A, V_A, K_B, V_B, POS = range(5)
FRONT = (K_A, V_A, K_B, POS)
RING_AT = {0: ((1, (3,)),), 1: ((2, (0, 1, 2, 4)),), 3: ((2, (3,)),), 5: ((3, (0, 1, 2, 4)),), 6: ((3, (3,)),), 9: ((4, (0, 1, 2, 4)),), 10: ((4, (3,)),)}
QUERY_AT = {0: 1, 3: 2, 5: 3}
DONE_AT = {14: 1, 12: 2, 11: 3}
TILES = NQ // TQ
STEPS = (NK // TK) * TILES


def kernel(
    q_in, k_in, v_in, p_in, out_ref,
    qall, kall, vall, qpos, kpos, vin, vt, ptile, acc, mx,
    cm_a, cm_b, al_a, al_b, s_a, s_b, p_a, p_b,
    osend, ssend, orecv, srecv, fsend, frecv,
    local, cell_s, cell_r, ring_s, ring_r, q_s, q_r, o_s, o_r, f_s, f_r,
):
    o, i = lax.axis_index("outer"), lax.axis_index("inner")
    xh, y = o // 4, lax.rem(o, 4)
    xl, z, core = i // 16, lax.rem(i // 2, 8), lax.rem(i, 2)

    def device(x, c):
        return (o, x * 16 + z * 2 + c)

    mates = {1: (xl, 1 - core), 2: (1 - xl, core), 3: (1 - xl, 1 - core)}
    theirs = {1: 1 - core, 2: 2 + core, 3: 3 - core}
    mine_at = {1: core, 2: 2 + core, 3: 2 + core}

    def ring(step):
        return (o, xl * 16 + lax.rem(z + step, 8) * 2 + core)

    def group(slot):
        dx, dy = OFFSETS[slot]
        return (lax.rem(xh + dx, 2) * 4 + lax.rem(y + dy, 4), i)

    def lanes(b, base=0):
        return pl.ds(pl.multiple_of(base + b * TOK, TOK), TOK)

    def remote(src, dst, send, recv, device):
        return pltpu.make_async_remote_copy(
            src_ref=src, dst_ref=dst, send_sem=send, recv_sem=recv, device_id=device, device_id_type=MESH
        )

    barrier = pltpu.get_barrier_semaphore()
    partners = [device(*mates[j]) for j in (1, 2, 3)] + [ring(1), ring(7)] + [group(s) for s in range(1, 8)]
    for partner in partners:
        pl.semaphore_signal(barrier, inc=1, device_id=partner, device_id_type=MESH)
    head = lanes(xl * 2 + core)
    loads = [
        pltpu.make_async_copy(v_in, vin, local.at[0]),
        pltpu.make_async_copy(k_in.at[:, head], kall.at[lanes(core, OWN * SUP), :], local.at[1]),
        pltpu.make_async_copy(q_in.at[:, head], qall.at[lanes(core), :], local.at[2]),
    ]
    for load in loads:
        load.start()
    ptile[...] = jnp.full(ptile.shape, p_in[0], jnp.int32)
    kpos[:, lanes(core, OWN * SUP)] = ptile[...]
    vall[DIM:, :] = jnp.ones((ROWS - DIM, NK), jnp.bfloat16)
    for load in loads:
        load.wait()
    for h in range(4):
        vt[h * DIM : (h + 1) * DIM, :] = vin[:, h * DIM : (h + 1) * DIM].T
    pl.semaphore_wait(barrier, len(partners))

    def trade(j, what, block):
        x, c = mates[j]
        to = x * 2 + c
        src, dst = (
            (k_in.at[:, lanes(to)], kall.at[lanes(block, OWN * SUP), :]),
            (vt.at[lanes(to), :], vall.at[pl.ds(0, DIM), lanes(block, OWN * SUP)]),
            (q_in.at[:, lanes(to)], qall.at[lanes(block), :]),
            (ptile, kpos.at[:, lanes(block, OWN * SUP)]),
        )[what]
        return remote(src, dst, cell_s.at[j - 1, what], cell_r.at[j - 1, what], device(x, c))

    for what in (0, 1):
        trade(1, what, mine_at[1]).start()
    for what in (3, 0, 2, 1):
        for j in (2, 3):
            trade(j, what, mine_at[j]).start()
        if what > 1:
            trade(1, what, mine_at[1]).start()
    vall[0:DIM, lanes(core, OWN * SUP)] = vt[head, :]

    def hop(way, dist, what):
        src = OWN if dist == 1 else 2 * (dist - 2) + way
        dst = 6 if dist == 4 else 2 * (dist - 1) + way
        lo, hi = ((0, SUP // 2), (0, SUP // 2), (SUP // 2, SUP), (SUP // 2, SUP), (0, SUP))[what]
        a, b = slice(src * SUP + lo, src * SUP + hi), slice(dst * SUP + lo, dst * SUP + hi)
        if what in (K_A, K_B):
            refs = kall.at[a, :], kall.at[b, :]
        elif what in (V_A, V_B):
            refs = vall.at[0:DIM, a], vall.at[0:DIM, b]
        else:
            refs = kpos.at[:, a], kpos.at[:, b]
        return remote(*refs, ring_s.at[way, dist - 1, what], ring_r.at[way, dist - 1, what], ring(1 if way == 0 else 7))

    def goes(way, dist, what):
        return dist < 4 or (dist == 4 and (what in (V_A, V_B)) == (way == 1))

    def arrive(dist, whats):
        for what in whats:
            for way in range(2):
                if goes(way, dist, what):
                    hop(way, dist, what).wait_recv()
                    if goes(way, dist + 1, what):
                        hop(way, dist + 1, what).start()

    def give(slot, at):
        a, b = slice(0, SUP), slice(at * SUP, (at + 1) * SUP)
        ka = slice(OWN * SUP, (OWN + 1) * SUP)
        return (
            remote(qall.at[a, :], qall.at[b, :], q_s.at[slot, 0], q_r.at[at, 0], group(slot)),
            remote(kpos.at[:, ka], qpos.at[:, b], q_s.at[slot, 1], q_r.at[at, 1], group(slot)),
        )

    def give_all(slots):
        for slot in slots:
            for copy in give(slot, BACK[slot]):
                copy.start()

    def traded(what, js):
        for j in js:
            trade(j, what, theirs[j]).wait_recv()

    def send_on(what):
        for way in range(2):
            hop(way, 1, what).start()

    traded(0, (1,))
    send_on(K_A)
    traded(1, (1,))
    send_on(V_A)
    traded(3, (1, 2, 3))
    send_on(POS)
    traded(0, (2, 3))
    send_on(K_B)
    traded(2, (1, 2, 3))
    give_all((2, 1, 3))
    traded(1, (2, 3))
    send_on(V_B)

    def queries_here(tile):
        for slot in range(tile * 2, tile * 2 + 2):
            if slot > 0:
                for copy in give(slot, slot):
                    copy.wait_recv()

    qpos[:, 0:SUP] = kpos[:, OWN * SUP :]
    acc[:, SUP:] = jnp.zeros((ROWS, NQ - SUP), jnp.float32)
    mx[:, SUP:] = jnp.full((8, NQ - SUP), LOW, jnp.float32)
    causal = lax.broadcasted_iota(jnp.int32, (TOK, TOK), 0) <= lax.broadcasted_iota(jnp.int32, (TOK, TOK), 1)
    for b in range(4):
        at = slice(b * TOK, (b + 1) * TOK)
        kat = slice(OWN * SUP + b * TOK, OWN * SUP + (b + 1) * TOK)
        s = lax.dot_general(kall[kat, :], qall[at, :], (((1,), (1,)), ((), ())), preferred_element_type=jnp.float32)
        s = jnp.where(causal, s, LOW)
        top = jnp.max(s, axis=0, keepdims=True)
        w = jnp.where(causal, jnp.exp2(s * SCALE - top * SCALE), 0.0).astype(jnp.bfloat16)
        acc[:, at] = jnp.dot(vall[:, kat], w, preferred_element_type=jnp.float32)
        mx[:, at] = jnp.broadcast_to(top, (8, TOK))

    S, W, CM, AL = (s_a, s_b), (p_a, p_b), (cm_a, cm_b), (al_a, al_b)

    def place(n):
        keys = jnp.where(n < 2, 0, jnp.where(n < 4, 1, jnp.where(n < 5, 0, jnp.where(n < 6, 1, jnp.where(n < 7, 0, jnp.where(n < 8, 1, jnp.where(n < 10, 2, jnp.where(n < 12, 3, jnp.where(n < 13, 2, jnp.where(n < 14, 3, jnp.where(n < 15, 2, 3)))))))))))
        tile = jnp.where(n < 1, 0, jnp.where(n < 2, 1, jnp.where(n < 3, 0, jnp.where(n < 4, 1, jnp.where(n < 6, 2, jnp.where(n < 9, 3, jnp.where(n < 10, 2, jnp.where(n < 11, 3, jnp.where(n < 12, 2, jnp.where(n < 14, 1, 0))))))))))
        return pl.multiple_of(keys * TK, TK), pl.multiple_of(tile * TQ, TQ)

    def kept(k0, q0, t, kb):
        kp = kpos[:, pl.ds(k0 + kb * TOK, TOK)]
        return jnp.concatenate([kp] * 4, axis=1) < qpos[:, pl.ds(q0 + t * SUP, SUP)]

    def scores(n, par):
        k0, q0 = place(n)
        for t in range(TQ // SUP):
            best = None
            for half in range(TK // SUP):
                s = lax.dot_general(
                    kall[pl.ds(k0 + half * SUP, SUP), :], qall[pl.ds(q0 + t * SUP, SUP), :],
                    (((1,), (1,)), ((), ())), preferred_element_type=jnp.float32,
                )
                S[par][half * SUP : (half + 1) * SUP, t * SUP : (t + 1) * SUP] = s
                for kb in range(4):
                    r = jnp.max(s[kb * TOK : (kb + 1) * TOK].reshape(TOK // 8, 8, SUP), axis=0)
                    r = jnp.where(kept(k0, q0, t, half * 4 + kb), r, LOW)
                    best = r if best is None else jnp.maximum(best, r)
            CM[par][:, t * SUP : (t + 1) * SUP] = best

    def weights(n, par):
        k0, q0 = place(n)
        qs = pl.ds(q0, TQ)
        old = mx[:, qs]
        new = jnp.maximum(old, jnp.max(CM[par][...], axis=0, keepdims=True))
        mx[:, qs] = new
        AL[par][...] = jnp.exp2((old - new) * SCALE)
        top = new * SCALE
        for t in range(TQ // SUP):
            ts = slice(t * SUP, (t + 1) * SUP)
            for kb in range(TK // TOK):
                less = jnp.where(kept(k0, q0, t, kb), top[:, ts], -LOW)
                ks = slice(kb * TOK, (kb + 1) * TOK)
                e = (S[par][ks, ts] * SCALE).reshape(TOK // 8, 8, SUP) - less[None]
                W[par][ks, ts] = jnp.exp2(e).reshape(TOK, SUP).astype(jnp.bfloat16)

    def sums(n, par):
        k0, q0 = place(n)
        for t in range(TQ // SUP):
            ts = slice(t * SUP, (t + 1) * SUP)
            qs = pl.ds(q0 + t * SUP, SUP)
            new = jnp.dot(vall[:, pl.ds(k0, TK)], W[par][:, ts], preferred_element_type=jnp.float32)
            acc[:, qs] = acc[:, qs] * AL[par][:1, ts] + new

    def stats(slot):
        at = slice(slot * SUP, (slot + 1) * SUP)
        m, l = mx[0:1, at], acc[DIM : DIM + 1, at]
        cut = [slice(b * TOK, (b + 1) * TOK) for b in range(4)]
        return jnp.concatenate([m[:, c] for c in cut] + [l[:, c] for c in cut], axis=0)

    def partial(slot, at):
        owner = group(slot)
        return (
            remote(osend.at[slot], orecv.at[at], o_s.at[slot, 0], o_r.at[at, 0], owner),
            remote(ssend.at[slot], srecv.at[at], o_s.at[slot, 1], o_r.at[at, 1], owner),
        )

    def send_partial(tile):
        for slot in (tile * 2 + 1, tile * 2):
            if slot > 0:
                osend[slot] = acc[0:DIM, slot * SUP : (slot + 1) * SUP].astype(jnp.bfloat16)
                ssend[slot] = stats(slot)
                for copy in partial(slot, BACK[slot]):
                    copy.start()

    queries_here(0)
    arrive(1, FRONT)
    give_all((4, 6, 5, 7))
    scores(jnp.int32(0), 0)
    p_b[...] = jnp.zeros_like(p_b)
    al_b[...] = jnp.ones_like(al_b)

    def before(n, parity):
        for at in range(parity, STEPS, 2):
            if at in RING_AT or at in QUERY_AT:

                @pl.when(n == at)
                def _(at=at):
                    for dist, whats in RING_AT.get(at, ()):
                        arrive(dist, whats)
                    if at in QUERY_AT:
                        queries_here(QUERY_AT[at])

    def after(n, parity):
        for at, tile in DONE_AT.items():
            if at % 2 == parity:

                @pl.when(n == at)
                def _(tile=tile):
                    send_partial(tile)

    def body(pair, carry):
        for par in range(2):
            n = 2 * pair + par
            before(n, par)
            scores(jnp.minimum(n + 1, STEPS - 1), 1 - par)
            weights(n, par)
            sums(jnp.maximum(n - 1, 0), 1 - par)
            after(n, par)
        return carry

    lax.fori_loop(0, STEPS // 2, body, 0)
    sums(jnp.int32(STEPS - 1), 1)
    send_partial(0)

    mine = stats(0)
    for slot in range(1, 8):
        for copy in partial(slot, slot):
            copy.wait_recv()
    all_stats = [mine] + [srecv[slot] for slot in range(1, 8)]
    best = functools.reduce(jnp.maximum, [st[0:4] for st in all_stats])
    factor = [jnp.exp2((st[0:4] - best) * SCALE) for st in all_stats]
    denom = functools.reduce(jnp.add, [st[4:8] * f for st, f in zip(all_stats, factor)])
    factor = [f / denom for f in factor]

    def home(block, x, c, at):
        return remote(fsend.at[block], frecv.at[at], f_s.at[block], f_r.at[at], device(x, c))

    for b in (2, 3, 0, 1):
        at = slice(b * TOK, (b + 1) * TOK)
        total = acc[0:DIM, at] * factor[0][b : b + 1]
        for slot in range(1, 8):
            total += orecv[slot, :, at].astype(jnp.float32) * factor[slot][b : b + 1]
        fsend[b] = total.T.astype(jnp.bfloat16)
        if b > 1:
            home(b, 1 - xl, b - 2, 2 + core).start()
    home(1 - core, xl, 1 - core, core).start()
    out_ref[:, head] = fsend[core]
    home(core, xl, 1 - core, 1 - core).wait_recv()
    out_ref[:, lanes(xl * 2 + 1 - core)] = frecv[1 - core]
    for c in range(2):
        home(2, 1 - xl, c, 2 + c).wait_recv()
        out_ref[:, lanes((1 - xl) * 2 + c)] = frecv[2 + c]

    for j in (1, 2, 3):
        for what in range(4):
            trade(j, what, mine_at[j]).wait_send()
    for b in (2, 3):
        home(b, 1 - xl, b - 2, 2 + core).wait_send()
    home(1 - core, xl, 1 - core, core).wait_send()
    for way in range(2):
        for dist in range(1, 5):
            for what in range(5):
                if goes(way, dist, what):
                    hop(way, dist, what).wait_send()
    for slot in range(1, 8):
        for copy in give(slot, BACK[slot]) + partial(slot, BACK[slot]):
            copy.wait_send()


def shards(queries, keys, values, block_pos):
    bf, f32, i32 = jnp.bfloat16, jnp.float32, jnp.int32
    vmem, dma = pltpu.VMEM, pltpu.SemaphoreType.DMA
    return pl.pallas_call(
        kernel,
        out_shape=jax.ShapeDtypeStruct(queries.shape, bf),
        in_specs=[pl.BlockSpec(memory_space=pl.ANY)] * 3 + [pl.BlockSpec(memory_space=pltpu.SMEM)],
        out_specs=pl.BlockSpec(memory_space=pltpu.VMEM),
        scratch_shapes=[
            vmem((NQ, DIM), bf), vmem((NK, DIM), bf), vmem((ROWS, NK), bf), vmem((8, NQ), i32), vmem((8, NK), i32),
            vmem((TOK, 4 * DIM), bf), vmem((4 * DIM, TOK), bf), vmem((8, TOK), i32), vmem((ROWS, NQ), f32), vmem((8, NQ), f32),
            vmem((8, TQ), f32), vmem((8, TQ), f32), vmem((8, TQ), f32), vmem((8, TQ), f32),
            vmem((TK, TQ), f32), vmem((TK, TQ), f32), vmem((TK, TQ), bf), vmem((TK, TQ), bf),
            vmem((8, DIM, SUP), bf), vmem((8, 8, TOK), f32), vmem((8, DIM, SUP), bf), vmem((8, 8, TOK), f32),
            vmem((4, TOK, DIM), bf), vmem((4, TOK, DIM), bf),
            dma((3,)), dma((3, 4)), dma((3, 4)), dma((2, 4, 5)), dma((2, 4, 5)), dma((8, 2)), dma((8, 2)), dma((8, 2)), dma((8, 2)),
            dma((4,)), dma((4,)),
        ],
        compiler_params=pltpu.CompilerParams(collective_id=0, has_side_effects=True, vmem_limit_bytes=56 << 20),
        cost_estimate=pl.CostEstimate(flops=NQ * NK * DIM * 4, bytes_accessed=1 << 20, transcendentals=NQ * NK),
        name="attend",
    )(queries, keys, values, block_pos)


def solution(mesh):
    spec = P(("outer", "inner"), None)
    return jax.shard_map(
        shards, mesh=mesh, in_specs=(spec, spec, spec, P(("outer", "inner"))), out_specs=spec, check_vma=False
    )
```

```python
import functools

import jax
import jax.numpy as jnp
from jax import lax
from jax.experimental import pallas as pl
from jax.experimental.pallas import tpu as pltpu
from jax.sharding import PartitionSpec as P

TOK = 128
DIM = 128
SUP = 4 * TOK
TQ = 1024
TK = 1024
ROWS = DIM + 16
NQ = 8 * SUP
NK = 8 * SUP
SCALE = DIM**-0.5 * 1.4426950408889634
LOW = -1e30
MESH = pl.DeviceIdType.MESH

OFFSETS = ((0, 0), (0, 1), (0, 3), (0, 2), (1, 0), (1, 1), (1, 3), (1, 2))
BACK = (0, 2, 1, 3, 4, 6, 5, 7)

OWN = 7
K_A, V_A, K_B, V_B, POS = range(5)
FRONT = (K_A, K_B, POS)
RING_AT = {1: ((1, (1, 3)), (2, (0, 2, 4))), 3: ((2, (1, 3)),), 6: ((3, (0, 2, 4)),), 8: ((3, (1, 3)),), 9: ((4, (0, 2, 4)),), 11: ((4, (1, 3)),)}
QUERY_AT = {0: 1, 3: 3, 4: 2}
DONE_AT = {14: 1, 11: 3, 12: 2}
TILES = NQ // TQ
STEPS = (NK // TK) * TILES


def kernel(
    q_in, k_in, v_in, p_in, out_ref,
    qall, kall, vall, qpos, kpos, qcode, kcode, marks, vin, vt, ptile, acc, mx,
    cm_a, cm_b, al_a, al_b, s_a, s_b, p_a, p_b,
    osend, ssend, orecv, srecv, fsend, frecv,
    local, cell_s, cell_r, ring_s, ring_r, q_s, q_r, o_s, o_r, f_s, f_r,
):
    o, i = lax.axis_index("outer"), lax.axis_index("inner")
    xh, y = o // 4, lax.rem(o, 4)
    xl, z, core = i // 16, lax.rem(i // 2, 8), lax.rem(i, 2)

    def device(x, c):
        return (o, x * 16 + z * 2 + c)

    mates = {1: (xl, 1 - core), 2: (1 - xl, core), 3: (1 - xl, 1 - core)}
    theirs = {1: 1 - core, 2: 2 + core, 3: 3 - core}
    mine_at = {1: core, 2: 2 + core, 3: 2 + core}

    def ring(step):
        return (o, xl * 16 + lax.rem(z + step, 8) * 2 + core)

    def group(slot):
        dx, dy = OFFSETS[slot]
        return (lax.rem(xh + dx, 2) * 4 + lax.rem(y + dy, 4), i)

    def lanes(b, base=0):
        return pl.ds(pl.multiple_of(base + b * TOK, TOK), TOK)

    def remote(src, dst, send, recv, device):
        return pltpu.make_async_remote_copy(
            src_ref=src, dst_ref=dst, send_sem=send, recv_sem=recv, device_id=device, device_id_type=MESH
        )

    barrier = pltpu.get_barrier_semaphore()
    partners = [device(*mates[j]) for j in (1, 2, 3)] + [ring(1), ring(7)] + [group(s) for s in range(1, 8)]
    for partner in partners:
        pl.semaphore_signal(barrier, inc=1, device_id=partner, device_id_type=MESH)
    head = lanes(xl * 2 + core)
    loads = [
        pltpu.make_async_copy(v_in, vin, local.at[0]),
        pltpu.make_async_copy(k_in.at[:, head], kall.at[lanes(core, OWN * SUP), :], local.at[1]),
        pltpu.make_async_copy(q_in.at[:, head], qall.at[lanes(core), :], local.at[2]),
    ]
    for load in loads:
        load.start()
    ptile[...] = jnp.full(ptile.shape, p_in[0], jnp.int32)
    marks[core] = ptile[...]
    vall[DIM:, 0:NK] = jnp.ones((ROWS - DIM, NK), jnp.bfloat16)
    vall[:, NK:] = jnp.zeros((ROWS, TK), jnp.bfloat16)
    for load in loads:
        load.wait()
    for h in range(4):
        vt[h * DIM : (h + 1) * DIM, :] = vin[:, h * DIM : (h + 1) * DIM].T
    pl.semaphore_wait(barrier, len(partners))

    def trade(j, what, block):
        x, c = mates[j]
        to = x * 2 + c
        src, dst = (
            (k_in.at[:, lanes(to)], kall.at[lanes(block, OWN * SUP), :]),
            (vt.at[lanes(to), :], vall.at[pl.ds(0, DIM), lanes(block, OWN * SUP)]),
            (q_in.at[:, lanes(to)], qall.at[lanes(block), :]),
            (ptile, marks.at[block]),
        )[what]
        return remote(src, dst, cell_s.at[j - 1, what], cell_r.at[j - 1, what], device(x, c))

    for what in (0, 1):
        trade(1, what, mine_at[1]).start()
    for what in (3, 0, 2, 1):
        for j in (2, 3):
            trade(j, what, mine_at[j]).start()
        if what > 1:
            trade(1, what, mine_at[1]).start()
    vall[0:DIM, lanes(core, OWN * SUP)] = vt[head, :]

    def hop(way, dist, what):
        src = OWN if dist == 1 else 2 * (dist - 2) + way
        dst = 6 if dist == 4 else 2 * (dist - 1) + way
        lo, hi = ((0, SUP // 2), (0, SUP // 2), (SUP // 2, SUP), (SUP // 2, SUP), (0, SUP))[what]
        a, b = slice(src * SUP + lo, src * SUP + hi), slice(dst * SUP + lo, dst * SUP + hi)
        if what in (K_A, K_B):
            refs = kall.at[a, :], kall.at[b, :]
        elif what in (V_A, V_B):
            refs = vall.at[0:DIM, a], vall.at[0:DIM, b]
        else:
            refs = kcode.at[src], kcode.at[dst]
        return remote(*refs, ring_s.at[way, dist - 1, what], ring_r.at[way, dist - 1, what], ring(1 if way == 0 else 7))

    def spread(wide, slot, code):
        for b in range(4):
            at = slice(slot * SUP + b * TOK, slot * SUP + (b + 1) * TOK)
            wide[:, at] = jnp.broadcast_to(code[slot, b : b + 1, :], (8, TOK))

    def goes(way, dist, what):
        return dist < 4 or (dist == 4 and (what in (V_A, V_B)) == (way == 1))

    def arrive(dist, whats):
        for what in whats:
            for way in range(2):
                if goes(way, dist, what):
                    hop(way, dist, what).wait_recv()
                    if goes(way, dist + 1, what):
                        hop(way, dist + 1, what).start()
                    if what == POS:
                        spread(kpos, 6 if dist == 4 else 2 * (dist - 1) + way, kcode)

    def give(slot, at):
        a, b = slice(0, SUP), slice(at * SUP, (at + 1) * SUP)
        return (
            remote(qall.at[a, :], qall.at[b, :], q_s.at[slot, 0], q_r.at[at, 0], group(slot)),
            remote(kcode.at[OWN], qcode.at[at], q_s.at[slot, 1], q_r.at[at, 1], group(slot)),
        )

    def pass_on(slot):
        at = 4 + BACK[slot]
        a, b = slice(4 * SUP, 5 * SUP), slice(at * SUP, (at + 1) * SUP)
        return (
            remote(qall.at[a, :], qall.at[b, :], q_s.at[4 + slot, 0], q_r.at[at, 0], group(slot)),
            remote(qcode.at[4], qcode.at[at], q_s.at[4 + slot, 1], q_r.at[at, 1], group(slot)),
        )

    def give_all(slots):
        for slot in slots:
            for copy in give(slot, BACK[slot]):
                copy.start()

    def traded(what, js):
        for j in js:
            trade(j, what, theirs[j]).wait_recv()

    def send_on(what):
        for way in range(2):
            hop(way, 1, what).start()

    traded(0, (1,))
    send_on(K_A)
    traded(3, (1, 2, 3))
    row = lax.broadcasted_iota(jnp.int32, (8, TOK), 0)
    kcode[OWN] = jnp.where(row == 0, marks[0], jnp.where(row == 1, marks[1], jnp.where(row == 2, marks[2], marks[3])))
    send_on(POS)
    spread(kpos, OWN, kcode)
    traded(0, (2, 3))
    send_on(K_B)
    traded(1, (1,))
    send_on(V_A)
    traded(2, (1, 2, 3))
    give_all((4, 2, 1, 3))
    traded(1, (2, 3))
    send_on(V_B)

    def queries_here(tile):
        for slot in range(tile * 2, tile * 2 + 2):
            if slot not in (0, 4):
                for copy in give(slot, slot):
                    copy.wait_recv()
            if slot > 0:
                spread(qpos, slot, qcode)

    qpos[:, 0:SUP] = kpos[:, OWN * SUP :]
    acc[:, SUP:] = jnp.zeros((ROWS, NQ - SUP), jnp.float32)
    mx[:, SUP:] = jnp.full((8, NQ - SUP), LOW, jnp.float32)
    causal = lax.broadcasted_iota(jnp.int32, (TOK, TOK), 0) <= lax.broadcasted_iota(jnp.int32, (TOK, TOK), 1)
    for b in range(4):
        at = slice(b * TOK, (b + 1) * TOK)
        kat = slice(OWN * SUP + b * TOK, OWN * SUP + (b + 1) * TOK)
        s = lax.dot_general(kall[kat, :], qall[at, :], (((1,), (1,)), ((), ())), preferred_element_type=jnp.float32)
        s = jnp.where(causal, s * SCALE, LOW)
        top = jnp.max(s, axis=0, keepdims=True)
        w = jnp.where(causal, jnp.exp2(s - top), 0.0).astype(jnp.bfloat16)
        acc[:, at] = jnp.dot(vall[:, kat], w, preferred_element_type=jnp.float32)
        mx[:, at] = jnp.broadcast_to(top, (8, TOK))

    S, W, CM, AL = (s_a, s_b), (p_a, p_b), (cm_a, cm_b), (al_a, al_b)

    def place(n):
        keys = jnp.where(n < 2, 0, jnp.where(n < 4, 1, jnp.where(n < 6, 0, jnp.where(n < 8, 1, jnp.where(n < 10, 2, jnp.where(n < 12, 3, jnp.where(n < 13, 2, jnp.where(n < 14, 3, jnp.where(n < 15, 2, 3)))))))))
        tile = jnp.where(n < 1, 0, jnp.where(n < 2, 1, jnp.where(n < 3, 0, jnp.where(n < 4, 1, jnp.where(n < 5, 3, jnp.where(n < 6, 2, jnp.where(n < 7, 3, jnp.where(n < 8, 2, jnp.where(n < 9, 3, jnp.where(n < 10, 2, jnp.where(n < 11, 3, jnp.where(n < 12, 2, jnp.where(n < 14, 1, 0)))))))))))))
        return pl.multiple_of(keys * TK, TK), pl.multiple_of(tile * TQ, TQ)

    def kept(k0, q0, t, kb):
        kp = kpos[:, pl.ds(k0 + kb * TOK, TOK)]
        return jnp.concatenate([kp] * 4, axis=1) < qpos[:, pl.ds(q0 + t * SUP, SUP)]

    def scores(n, par):
        k0, q0 = place(n)
        for t in range(TQ // SUP):
            best = None
            for half in range(TK // SUP):
                s = lax.dot_general(
                    kall[pl.ds(k0 + half * SUP, SUP), :], qall[pl.ds(q0 + t * SUP, SUP), :],
                    (((1,), (1,)), ((), ())), preferred_element_type=jnp.float32,
                ) * SCALE
                S[par][half * SUP : (half + 1) * SUP, t * SUP : (t + 1) * SUP] = s
                for kb in range(4):
                    r = jnp.max(s[kb * TOK : (kb + 1) * TOK].reshape(TOK // 8, 8, SUP), axis=0)
                    r = jnp.where(kept(k0, q0, t, half * 4 + kb), r, LOW)
                    best = r if best is None else jnp.maximum(best, r)
            CM[par][:, t * SUP : (t + 1) * SUP] = best

    def weights(n, par):
        k0, q0 = place(n)
        qs = pl.ds(q0, TQ)
        old = mx[:, qs]
        new = jnp.maximum(old, jnp.max(CM[par][...], axis=0, keepdims=True))
        mx[:, qs] = new
        AL[par][...] = jnp.exp2(old - new)
        for t in range(TQ // SUP):
            ts = slice(t * SUP, (t + 1) * SUP)
            for kb in range(TK // TOK):
                less = jnp.where(kept(k0, q0, t, kb), new[:, ts], -LOW)
                ks = slice(kb * TOK, (kb + 1) * TOK)
                e = S[par][ks, ts].reshape(TOK // 8, 8, SUP) - less[None]
                W[par][ks, ts] = jnp.exp2(e).reshape(TOK, SUP).astype(jnp.bfloat16)

    def sums(n, par):
        k0, q0 = place(jnp.maximum(n, 0))
        k0 = pl.multiple_of(jnp.where(n < 0, NK, k0), TK)
        for t in range(TQ // SUP):
            ts = slice(t * SUP, (t + 1) * SUP)
            qs = pl.ds(q0 + t * SUP, SUP)
            new = jnp.dot(vall[:, pl.ds(k0, TK)], W[par][:, ts], preferred_element_type=jnp.float32)
            acc[:, qs] = acc[:, qs] * AL[par][:1, ts] + new

    def stats(slot):
        at = slice(slot * SUP, (slot + 1) * SUP)
        m, l = mx[0:1, at], acc[DIM : DIM + 1, at]
        cut = [slice(b * TOK, (b + 1) * TOK) for b in range(4)]
        return jnp.concatenate([m[:, c] for c in cut] + [l[:, c] for c in cut], axis=0)

    def partial(slot, at):
        owner = group(slot)
        return (
            remote(osend.at[slot], orecv.at[at], o_s.at[slot, 0], o_r.at[at, 0], owner),
            remote(ssend.at[slot], srecv.at[at], o_s.at[slot, 1], o_r.at[at, 1], owner),
        )

    def send_partial(tile):
        for slot in (tile * 2 + 1, tile * 2):
            if slot > 0:
                osend[slot] = acc[0:DIM, slot * SUP : (slot + 1) * SUP].astype(jnp.bfloat16)
                ssend[slot] = stats(slot)
                for copy in partial(slot, BACK[slot]):
                    copy.start()

    queries_here(0)
    for copy in give(4, 4):
        copy.wait_recv()
    for slot in (1, 3, 2):
        for copy in pass_on(slot):
            copy.start()
    arrive(1, FRONT)
    scores(jnp.int32(0), 0)
    p_b[...] = jnp.zeros_like(p_b)
    al_b[...] = jnp.ones_like(al_b)

    def before(n, parity):
        for at in range(parity, STEPS, 2):
            if at in RING_AT or at in QUERY_AT:

                @pl.when(n == at)
                def _(at=at):
                    for dist, whats in RING_AT.get(at, ()):
                        arrive(dist, whats)
                    if at in QUERY_AT:
                        queries_here(QUERY_AT[at])

    def after(n, parity):
        for at, tile in DONE_AT.items():
            if at % 2 == parity:

                @pl.when(n == at)
                def _(tile=tile):
                    send_partial(tile)

    def body(pair, carry):
        for par in range(2):
            n = 2 * pair + par
            before(n, par)
            scores(jnp.minimum(n + 1, STEPS - 1), 1 - par)
            weights(n, par)
            sums(n - 1, 1 - par)
            after(n, par)
        return carry

    lax.fori_loop(0, STEPS // 2, body, 0)
    sums(jnp.int32(STEPS - 1), 1)
    send_partial(0)

    mine = stats(0)
    for slot in range(1, 8):
        for copy in partial(slot, slot):
            copy.wait_recv()
    all_stats = [mine] + [srecv[slot] for slot in range(1, 8)]
    best = functools.reduce(jnp.maximum, [st[0:4] for st in all_stats])
    factor = [jnp.exp2(st[0:4] - best) for st in all_stats]
    denom = functools.reduce(jnp.add, [st[4:8] * f for st, f in zip(all_stats, factor)])
    factor = [f / denom for f in factor]

    def home(block, x, c, at):
        return remote(fsend.at[block], frecv.at[at], f_s.at[block], f_r.at[at], device(x, c))

    for b in (2, 3, 0, 1):
        at = slice(b * TOK, (b + 1) * TOK)
        total = acc[0:DIM, at] * factor[0][b : b + 1]
        for slot in range(1, 8):
            total += orecv[slot, :, at].astype(jnp.float32) * factor[slot][b : b + 1]
        fsend[b] = total.T.astype(jnp.bfloat16)
        if b > 1:
            home(b, 1 - xl, b - 2, 2 + core).start()
    home(1 - core, xl, 1 - core, core).start()
    out_ref[:, head] = fsend[core]
    home(core, xl, 1 - core, 1 - core).wait_recv()
    out_ref[:, lanes(xl * 2 + 1 - core)] = frecv[1 - core]
    for c in range(2):
        home(2, 1 - xl, c, 2 + c).wait_recv()
        out_ref[:, lanes((1 - xl) * 2 + c)] = frecv[2 + c]

    for j in (1, 2, 3):
        for what in range(4):
            trade(j, what, mine_at[j]).wait_send()
    for b in (2, 3):
        home(b, 1 - xl, b - 2, 2 + core).wait_send()
    home(1 - core, xl, 1 - core, core).wait_send()
    for way in range(2):
        for dist in range(1, 5):
            for what in range(5):
                if goes(way, dist, what):
                    hop(way, dist, what).wait_send()
    for slot in range(1, 8):
        for copy in (give(slot, BACK[slot]) if slot < 5 else pass_on(slot - 4)) + partial(slot, BACK[slot]):
            copy.wait_send()


def shards(queries, keys, values, block_pos):
    bf, f32, i32 = jnp.bfloat16, jnp.float32, jnp.int32
    vmem, dma = pltpu.VMEM, pltpu.SemaphoreType.DMA
    return pl.pallas_call(
        kernel,
        out_shape=jax.ShapeDtypeStruct(queries.shape, bf),
        in_specs=[pl.BlockSpec(memory_space=pl.ANY)] * 3 + [pl.BlockSpec(memory_space=pltpu.SMEM)],
        out_specs=pl.BlockSpec(memory_space=pltpu.VMEM),
        scratch_shapes=[
            vmem((NQ, DIM), bf), vmem((NK, DIM), bf), vmem((ROWS, NK + TK), bf), vmem((8, NQ), i32), vmem((8, NK), i32), vmem((8, 8, TOK), i32), vmem((8, 8, TOK), i32), vmem((4, 8, TOK), i32),
            vmem((TOK, 4 * DIM), bf), vmem((4 * DIM, TOK), bf), vmem((8, TOK), i32), vmem((ROWS, NQ), f32), vmem((8, NQ), f32),
            vmem((8, TQ), f32), vmem((8, TQ), f32), vmem((8, TQ), f32), vmem((8, TQ), f32),
            vmem((TK, TQ), f32), vmem((TK, TQ), f32), vmem((TK, TQ), bf), vmem((TK, TQ), bf),
            vmem((8, DIM, SUP), bf), vmem((8, 8, TOK), f32), vmem((8, DIM, SUP), bf), vmem((8, 8, TOK), f32),
            vmem((4, TOK, DIM), bf), vmem((4, TOK, DIM), bf),
            dma((3,)), dma((3, 4)), dma((3, 4)), dma((2, 4, 5)), dma((2, 4, 5)), dma((8, 2)), dma((8, 2)), dma((8, 2)), dma((8, 2)),
            dma((4,)), dma((4,)),
        ],
        compiler_params=pltpu.CompilerParams(collective_id=0, has_side_effects=True, vmem_limit_bytes=56 << 20),
        cost_estimate=pl.CostEstimate(flops=NQ * NK * DIM * 4, bytes_accessed=1 << 20, transcendentals=NQ * NK),
        name="attend",
    )(queries, keys, values, block_pos)


def solution(mesh):
    spec = P(("outer", "inner"), None)
    return jax.shard_map(
        shards, mesh=mesh, in_specs=(spec, spec, spec, P(("outer", "inner"))), out_specs=spec, check_vma=False
    )
```

```python
import functools

import jax
import jax.numpy as jnp
from jax import lax
from jax.experimental import pallas as pl
from jax.experimental.pallas import tpu as pltpu
from jax.sharding import PartitionSpec as P

TOK = 128
DIM = 128
SUP = 4 * TOK
TQ = 1024
TK = 1024
ROWS = DIM + 16
NQ = 8 * SUP
NK = 8 * SUP
SCALE = DIM**-0.5 * 1.4426950408889634
LOW = -1e30
MESH = pl.DeviceIdType.MESH

OFFSETS = ((0, 0), (0, 1), (0, 3), (0, 2), (1, 0), (1, 1), (1, 3), (1, 2))
BACK = (0, 2, 1, 3, 4, 6, 5, 7)

OWN = 7
K_A, V_A, K_B, V_B, POS = range(5)
FRONT = (K_A, K_B, POS)
RING_AT = {1: ((1, (1, 3)), (2, (0, 2, 4))), 3: ((2, (1, 3)),), 6: ((3, (0, 2, 4)),), 8: ((3, (1, 3)),), 9: ((4, (0, 2, 4)),), 11: ((4, (1, 3)),)}
QUERY_AT = {0: 1, 3: 3, 4: 2}
DONE_AT = {14: 1, 11: 3, 12: 2}
TILES = NQ // TQ
STEPS = (NK // TK) * TILES


def kernel(
    q_in, k_in, v_in, p_in, out_ref,
    qall, kall, vall, qpos, kpos, qcode, kcode, marks, vin, vt, ptile, acc, mx,
    cm_a, cm_b, al_a, al_b, s_a, s_b, p_a, p_b,
    osend, ssend, orecv, srecv, fsend, frecv,
    local, cell_s, cell_r, ring_s, ring_r, q_s, q_r, o_s, o_r, f_s, f_r,
):
    o, i = lax.axis_index("outer"), lax.axis_index("inner")
    xh, y = o // 4, lax.rem(o, 4)
    xl, z, core = i // 16, lax.rem(i // 2, 8), lax.rem(i, 2)

    def device(x, c):
        return (o, x * 16 + z * 2 + c)

    mates = {1: (xl, 1 - core), 2: (1 - xl, core), 3: (1 - xl, 1 - core)}
    theirs = {1: 1 - core, 2: 2 + core, 3: 3 - core}
    mine_at = {1: core, 2: 2 + core, 3: 2 + core}

    def ring(step):
        return (o, xl * 16 + lax.rem(z + step, 8) * 2 + core)

    def group(slot):
        dx, dy = OFFSETS[slot]
        return (lax.rem(xh + dx, 2) * 4 + lax.rem(y + dy, 4), i)

    def lanes(b, base=0):
        return pl.ds(pl.multiple_of(base + b * TOK, TOK), TOK)

    def remote(src, dst, send, recv, device):
        return pltpu.make_async_remote_copy(
            src_ref=src, dst_ref=dst, send_sem=send, recv_sem=recv, device_id=device, device_id_type=MESH
        )

    barrier = pltpu.get_barrier_semaphore()
    partners = [device(*mates[j]) for j in (1, 2, 3)] + [ring(1), ring(7)] + [group(s) for s in range(1, 8)]
    for partner in partners:
        pl.semaphore_signal(barrier, inc=1, device_id=partner, device_id_type=MESH)
    head = lanes(xl * 2 + core)
    loads = [
        pltpu.make_async_copy(v_in, vin, local.at[0]),
        pltpu.make_async_copy(k_in.at[:, head], kall.at[lanes(core, OWN * SUP), :], local.at[1]),
        pltpu.make_async_copy(q_in.at[:, head], qall.at[lanes(core), :], local.at[2]),
    ]
    for load in loads:
        load.start()
    ptile[...] = jnp.full(ptile.shape, p_in[0], jnp.int32)
    marks[core] = ptile[...]
    vall[DIM:, 0:NK] = jnp.ones((ROWS - DIM, NK), jnp.bfloat16)
    vall[:, NK:] = jnp.zeros((ROWS, TK), jnp.bfloat16)
    for load in loads:
        load.wait()
    for h in range(4):
        vt[h * DIM : (h + 1) * DIM, :] = vin[:, h * DIM : (h + 1) * DIM].T
    pl.semaphore_wait(barrier, len(partners))

    def trade(j, what, block):
        x, c = mates[j]
        to = x * 2 + c
        src, dst = (
            (k_in.at[:, lanes(to)], kall.at[lanes(block, OWN * SUP), :]),
            (vt.at[lanes(to), :], vall.at[pl.ds(0, DIM), lanes(block, OWN * SUP)]),
            (q_in.at[:, lanes(to)], qall.at[lanes(block), :]),
            (ptile, marks.at[block]),
        )[what]
        return remote(src, dst, cell_s.at[j - 1, what], cell_r.at[j - 1, what], device(x, c))

    for what in (0, 1):
        trade(1, what, mine_at[1]).start()
    for what in (3, 0, 2, 1):
        for j in (2, 3):
            trade(j, what, mine_at[j]).start()
        if what > 1:
            trade(1, what, mine_at[1]).start()
    vall[0:DIM, lanes(core, OWN * SUP)] = vt[head, :]

    def hop(way, dist, what):
        src = OWN if dist == 1 else 2 * (dist - 2) + way
        dst = 6 if dist == 4 else 2 * (dist - 1) + way
        lo, hi = ((0, SUP // 2), (0, SUP // 2), (SUP // 2, SUP), (SUP // 2, SUP), (0, SUP))[what]
        a, b = slice(src * SUP + lo, src * SUP + hi), slice(dst * SUP + lo, dst * SUP + hi)
        if what in (K_A, K_B):
            refs = kall.at[a, :], kall.at[b, :]
        elif what in (V_A, V_B):
            refs = vall.at[0:DIM, a], vall.at[0:DIM, b]
        else:
            refs = kcode.at[src], kcode.at[dst]
        return remote(*refs, ring_s.at[way, dist - 1, what], ring_r.at[way, dist - 1, what], ring(1 if way == 0 else 7))

    def spread(wide, slot, code):
        for b in range(4):
            at = slice(slot * SUP + b * TOK, slot * SUP + (b + 1) * TOK)
            wide[:, at] = jnp.broadcast_to(code[slot, b : b + 1, :], (8, TOK))

    def goes(way, dist, what):
        return dist < 4 or (dist == 4 and (what in (V_A, V_B)) == (way == 1))

    def arrive(dist, whats):
        for what in whats:
            for way in range(2):
                if goes(way, dist, what):
                    hop(way, dist, what).wait_recv()
                    if goes(way, dist + 1, what):
                        hop(way, dist + 1, what).start()
                    if what == POS:
                        spread(kpos, 6 if dist == 4 else 2 * (dist - 1) + way, kcode)

    def give(slot, at):
        a, b = slice(0, SUP), slice(at * SUP, (at + 1) * SUP)
        return (
            remote(qall.at[a, :], qall.at[b, :], q_s.at[slot, 0], q_r.at[at, 0], group(slot)),
            remote(kcode.at[OWN], qcode.at[at], q_s.at[slot, 1], q_r.at[at, 1], group(slot)),
        )

    def pass_on(slot):
        at = 4 + BACK[slot]
        a, b = slice(4 * SUP, 5 * SUP), slice(at * SUP, (at + 1) * SUP)
        return (
            remote(qall.at[a, :], qall.at[b, :], q_s.at[4 + slot, 0], q_r.at[at, 0], group(slot)),
            remote(qcode.at[4], qcode.at[at], q_s.at[4 + slot, 1], q_r.at[at, 1], group(slot)),
        )

    def give_all(slots):
        for slot in slots:
            for copy in give(slot, BACK[slot]):
                copy.start()

    def traded(what, js):
        for j in js:
            trade(j, what, theirs[j]).wait_recv()

    def send_on(what):
        for way in range(2):
            hop(way, 1, what).start()

    traded(0, (1,))
    send_on(K_A)
    traded(3, (1, 2, 3))
    row = lax.broadcasted_iota(jnp.int32, (8, TOK), 0)
    kcode[OWN] = jnp.where(row == 0, marks[0], jnp.where(row == 1, marks[1], jnp.where(row == 2, marks[2], marks[3])))
    send_on(POS)
    spread(kpos, OWN, kcode)
    traded(0, (2, 3))
    send_on(K_B)
    traded(1, (1,))
    send_on(V_A)
    traded(2, (1, 2, 3))
    give_all((4, 2, 1, 3))
    traded(1, (2, 3))
    send_on(V_B)

    def queries_here(tile):
        for slot in range(tile * 2, tile * 2 + 2):
            if slot not in (0, 4):
                for copy in give(slot, slot):
                    copy.wait_recv()
            if slot > 0:
                spread(qpos, slot, qcode)

    qpos[:, 0:SUP] = kpos[:, OWN * SUP :]
    acc[:, SUP:] = jnp.zeros((ROWS, NQ - SUP), jnp.float32)
    mx[:, SUP:] = jnp.full((8, NQ - SUP), LOW, jnp.float32)
    causal = lax.broadcasted_iota(jnp.int32, (TOK, TOK), 0) <= lax.broadcasted_iota(jnp.int32, (TOK, TOK), 1)
    for b in range(4):
        at = slice(b * TOK, (b + 1) * TOK)
        kat = slice(OWN * SUP + b * TOK, OWN * SUP + (b + 1) * TOK)
        s = lax.dot_general(kall[kat, :], qall[at, :], (((1,), (1,)), ((), ())), preferred_element_type=jnp.float32)
        s = jnp.where(causal, s * SCALE, LOW)
        top = jnp.max(s, axis=0, keepdims=True)
        w = jnp.where(causal, jnp.exp2(s - top), 0.0).astype(jnp.bfloat16)
        acc[:, at] = jnp.dot(vall[:, kat], w, preferred_element_type=jnp.float32)
        mx[:, at] = jnp.broadcast_to(top, (8, TOK))

    S, W, CM, AL = (s_a, s_b), (p_a, p_b), (cm_a, cm_b), (al_a, al_b)

    def place(n):
        keys = jnp.where(n < 2, 0, jnp.where(n < 4, 1, jnp.where(n < 6, 0, jnp.where(n < 8, 1, jnp.where(n < 10, 2, jnp.where(n < 12, 3, jnp.where(n < 13, 2, jnp.where(n < 14, 3, jnp.where(n < 15, 2, 3)))))))))
        tile = jnp.where(n < 1, 0, jnp.where(n < 2, 1, jnp.where(n < 3, 0, jnp.where(n < 4, 1, jnp.where(n < 5, 3, jnp.where(n < 6, 2, jnp.where(n < 7, 3, jnp.where(n < 8, 2, jnp.where(n < 9, 3, jnp.where(n < 10, 2, jnp.where(n < 11, 3, jnp.where(n < 12, 2, jnp.where(n < 14, 1, 0)))))))))))))
        return pl.multiple_of(keys * TK, TK), pl.multiple_of(tile * TQ, TQ)

    def kept(k0, q0, t, kb):
        kp = kpos[:, pl.ds(k0 + kb * TOK, TOK)]
        return jnp.concatenate([kp] * 4, axis=1) < qpos[:, pl.ds(q0 + t * SUP, SUP)]

    def scores(n, par):
        k0, q0 = place(n)
        for t in range(TQ // SUP):
            best = None
            for half in range(TK // SUP):
                s = lax.dot_general(
                    kall[pl.ds(k0 + half * SUP, SUP), :], qall[pl.ds(q0 + t * SUP, SUP), :],
                    (((1,), (1,)), ((), ())), preferred_element_type=jnp.float32,
                ) * SCALE
                S[par][half * SUP : (half + 1) * SUP, t * SUP : (t + 1) * SUP] = s
                for kb in range(4):
                    r = jnp.max(s[kb * TOK : (kb + 1) * TOK].reshape(TOK // 8, 8, SUP), axis=0)
                    r = jnp.where(kept(k0, q0, t, half * 4 + kb), r, LOW)
                    best = r if best is None else jnp.maximum(best, r)
            CM[par][:, t * SUP : (t + 1) * SUP] = best

    def weights(n, par):
        k0, q0 = place(n)
        qs = pl.ds(q0, TQ)
        old = mx[:, qs]
        new = jnp.maximum(old, jnp.max(CM[par][...], axis=0, keepdims=True))
        mx[:, qs] = new
        AL[par][...] = jnp.exp2(old - new)
        for t in range(TQ // SUP):
            ts = slice(t * SUP, (t + 1) * SUP)
            for kb in range(TK // TOK):
                less = jnp.where(kept(k0, q0, t, kb), new[:, ts], -LOW)
                ks = slice(kb * TOK, (kb + 1) * TOK)
                e = S[par][ks, ts].reshape(TOK // 8, 8, SUP) - less[None]
                W[par][ks, ts] = jnp.exp2(e).reshape(TOK, SUP).astype(jnp.bfloat16)

    def sums(n, par):
        k0, q0 = place(jnp.maximum(n, 0))
        k0 = pl.multiple_of(jnp.where(n < 0, NK, k0), TK)
        for t in range(TQ // SUP):
            ts = slice(t * SUP, (t + 1) * SUP)
            qs = pl.ds(q0 + t * SUP, SUP)
            new = jnp.dot(vall[:, pl.ds(k0, TK)], W[par][:, ts], preferred_element_type=jnp.float32)
            acc[:, qs] = acc[:, qs] * AL[par][:1, ts] + new

    def stats(slot):
        at = slice(slot * SUP, (slot + 1) * SUP)
        m, l = mx[0:1, at], acc[DIM : DIM + 1, at]
        cut = [slice(b * TOK, (b + 1) * TOK) for b in range(4)]
        return jnp.concatenate([m[:, c] for c in cut] + [l[:, c] for c in cut], axis=0)

    def partial(slot, at):
        owner = group(slot)
        return (
            remote(osend.at[slot], orecv.at[at], o_s.at[slot, 0], o_r.at[at, 0], owner),
            remote(ssend.at[slot], srecv.at[at], o_s.at[slot, 1], o_r.at[at, 1], owner),
        )

    def send_partial(tile):
        for slot in (tile * 2 + 1, tile * 2):
            if slot > 0:
                osend[slot] = acc[0:DIM, slot * SUP : (slot + 1) * SUP].astype(jnp.bfloat16)
                ssend[slot] = stats(slot)
                for copy in partial(slot, BACK[slot]):
                    copy.start()

    queries_here(0)
    for copy in give(4, 4):
        copy.wait_recv()
    for slot in (1, 3, 2):
        for copy in pass_on(slot):
            copy.start()
    arrive(1, FRONT)
    scores(jnp.int32(0), 0)
    p_b[...] = jnp.zeros_like(p_b)
    al_b[...] = jnp.ones_like(al_b)

    def before(n, parity):
        for at in range(parity, STEPS, 2):
            if at in RING_AT or at in QUERY_AT:

                @pl.when(n == at)
                def _(at=at):
                    for dist, whats in RING_AT.get(at, ()):
                        arrive(dist, whats)
                    if at in QUERY_AT:
                        queries_here(QUERY_AT[at])

    def after(n, parity):
        for at, tile in DONE_AT.items():
            if at % 2 == parity:

                @pl.when(n == at)
                def _(tile=tile):
                    send_partial(tile)

    def body(pair, carry):
        for par in range(2):
            n = 2 * pair + par
            before(n, par)
            weights(n, par)
            sums(n - 1, 1 - par)
            scores(jnp.minimum(n + 1, STEPS - 1), 1 - par)
            after(n, par)
        return carry

    lax.fori_loop(0, STEPS // 2, body, 0)
    sums(jnp.int32(STEPS - 1), 1)
    send_partial(0)

    mine = stats(0)
    for slot in range(1, 8):
        for copy in partial(slot, slot):
            copy.wait_recv()
    all_stats = [mine] + [srecv[slot] for slot in range(1, 8)]
    best = functools.reduce(jnp.maximum, [st[0:4] for st in all_stats])
    factor = [jnp.exp2(st[0:4] - best) for st in all_stats]
    denom = functools.reduce(jnp.add, [st[4:8] * f for st, f in zip(all_stats, factor)])
    factor = [f / denom for f in factor]

    def home(block, x, c, at):
        return remote(fsend.at[block], frecv.at[at], f_s.at[block], f_r.at[at], device(x, c))

    for b in (2, 3, 0, 1):
        at = slice(b * TOK, (b + 1) * TOK)
        total = acc[0:DIM, at] * factor[0][b : b + 1]
        for slot in range(1, 8):
            total += orecv[slot, :, at].astype(jnp.float32) * factor[slot][b : b + 1]
        fsend[b] = total.T.astype(jnp.bfloat16)
        if b > 1:
            home(b, 1 - xl, b - 2, 2 + core).start()
    home(1 - core, xl, 1 - core, core).start()
    out_ref[:, head] = fsend[core]
    home(core, xl, 1 - core, 1 - core).wait_recv()
    out_ref[:, lanes(xl * 2 + 1 - core)] = frecv[1 - core]
    for c in range(2):
        home(2, 1 - xl, c, 2 + c).wait_recv()
        out_ref[:, lanes((1 - xl) * 2 + c)] = frecv[2 + c]

    for j in (1, 2, 3):
        for what in range(4):
            trade(j, what, mine_at[j]).wait_send()
    for b in (2, 3):
        home(b, 1 - xl, b - 2, 2 + core).wait_send()
    home(1 - core, xl, 1 - core, core).wait_send()
    for way in range(2):
        for dist in range(1, 5):
            for what in range(5):
                if goes(way, dist, what):
                    hop(way, dist, what).wait_send()
    for slot in range(1, 8):
        for copy in (give(slot, BACK[slot]) if slot < 5 else pass_on(slot - 4)) + partial(slot, BACK[slot]):
            copy.wait_send()


def shards(queries, keys, values, block_pos):
    bf, f32, i32 = jnp.bfloat16, jnp.float32, jnp.int32
    vmem, dma = pltpu.VMEM, pltpu.SemaphoreType.DMA
    return pl.pallas_call(
        kernel,
        out_shape=jax.ShapeDtypeStruct(queries.shape, bf),
        in_specs=[pl.BlockSpec(memory_space=pl.ANY)] * 3 + [pl.BlockSpec(memory_space=pltpu.SMEM)],
        out_specs=pl.BlockSpec(memory_space=pltpu.VMEM),
        scratch_shapes=[
            vmem((NQ, DIM), bf), vmem((NK, DIM), bf), vmem((ROWS, NK + TK), bf), vmem((8, NQ), i32), vmem((8, NK), i32), vmem((8, 8, TOK), i32), vmem((8, 8, TOK), i32), vmem((4, 8, TOK), i32),
            vmem((TOK, 4 * DIM), bf), vmem((4 * DIM, TOK), bf), vmem((8, TOK), i32), vmem((ROWS, NQ), f32), vmem((8, NQ), f32),
            vmem((8, TQ), f32), vmem((8, TQ), f32), vmem((8, TQ), f32), vmem((8, TQ), f32),
            vmem((TK, TQ), f32), vmem((TK, TQ), f32), vmem((TK, TQ), bf), vmem((TK, TQ), bf),
            vmem((8, DIM, SUP), bf), vmem((8, 8, TOK), f32), vmem((8, DIM, SUP), bf), vmem((8, 8, TOK), f32),
            vmem((4, TOK, DIM), bf), vmem((4, TOK, DIM), bf),
            dma((3,)), dma((3, 4)), dma((3, 4)), dma((2, 4, 5)), dma((2, 4, 5)), dma((8, 2)), dma((8, 2)), dma((8, 2)), dma((8, 2)),
            dma((4,)), dma((4,)),
        ],
        compiler_params=pltpu.CompilerParams(collective_id=0, has_side_effects=True, vmem_limit_bytes=56 << 20),
        cost_estimate=pl.CostEstimate(flops=NQ * NK * DIM * 4, bytes_accessed=1 << 20, transcendentals=NQ * NK),
        name="attend",
    )(queries, keys, values, block_pos)


def solution(mesh):
    spec = P(("outer", "inner"), None)
    return jax.shard_map(
        shards, mesh=mesh, in_specs=(spec, spec, spec, P(("outer", "inner"))), out_specs=spec, check_vma=False
    )
```
